256 devices in a mesh: pose: 128 (over x, y, z), row: 2 (over core).
Axes of the slice: x: 4, y: 4, z: 8, core: 2. Of those that a mesh axis runs over, the one named last changes fastest.
Arguments:
- images: bfloat16 [16384, 65536], P('pose', 'row'), may hold values from -6 to 6
- routes: int32 [16384, 1], P('pose'), may hold values from 0 to 127; in each aligned block of 128 rows (0 to 127, 128 to 255, ...) at most 2 rows name the same one
- orientations: int32 [16384], P('pose'), may hold values from 0 to 3
- groups: int32 [16384], P('pose'), may hold values from 0 to 7
- counts: int32 [128], P('pose'), may hold values from 64 to 128, as said below
- defocus: float32 [8], replicated, may hold values from 40 to 160
- projections: bfloat16 [128, 16, 65536], P('pose', None, 'row'), may hold values from -0.0234375 to 0.0234375
Outputs:
- coords: float32 [16384, 16], P('pose')
- basis: bfloat16 [128, 65536, 64], P('pose', 'row')
The draws below stay inside these ranges and needn't reach their ends.
Inputs may be any that keep to these rules, and one draw needn't show every extreme that they name: `routes`: in the rows of one source device no block is named more than 2 times, and some block exactly 2 times. `counts`: some source device is full in every draw.
All inputs are finite; a program needn't handle non-finite values.
Results may differ from the reference program's by a relative error of at most 0.0064.
Values may be sent and summed in bfloat16 or wider, within the bound.
No kernel may reach another device: no remote copies, remote signals or barrier semaphores. Data moves between devices by JAX's collectives and lax.ppermute only.
A program may use at most 128 MiB of HBM per device.

```python
import math
import jax
import jax.numpy as jnp
import numpy as np
from jax import lax

BOX = 256
K = 16
ORIENT = 4
GROUPS = 8
PART_DEV = 128
PARTICLES = 16384
CAP = 2
SLOTS = 256
PANEL = 64
N_POSE = 128


def draw_counts(key, part):
    key = jax.random.fold_in(key, 7)
    first, second = jax.random.split(key)
    base = jax.random.randint(first, (N_POSE,), PART_DEV // 2, PART_DEV + 1)
    filled = jax.random.randint(second, (), 0, N_POSE)
    return jnp.where(jnp.arange(N_POSE) == filled, PART_DEV, base).astype(jnp.int32)


def place_ends(drawn, rng, least, top_value):
    longest = drawn.shape.index(max(drawn.shape))
    spots = []
    for shift in (0, 1):
        where = [jax.random.randint(jax.random.fold_in(rng, axis), (), 0, length) for axis, length in enumerate(drawn.shape)]
        where[longest] = (where[longest] + shift) % drawn.shape[longest]
        spots.append(tuple(where))
    return drawn.at[spots[0]].set(least).at[spots[1]].set(top_value)


def block_scale(stream_key, extent, shards, least, high):
    factor_of = 1.0
    for axis_at, parts in shards:
        steps = jax.random.uniform(jax.random.fold_in(jax.random.fold_in(stream_key, 6), axis_at), (parts,), jnp.float32, least / len(shards), high / len(shards))
        factor_of = factor_of * jnp.repeat(jnp.exp(steps), extent[axis_at] // parts).reshape((-1,) + (1,) * (len(extent) - 1 - axis_at))
    return factor_of


def shared_out(stream_key, own, number, rows, count, top, reach, skew):
    order = jax.random.permutation(stream_key, count)
    packed, ordinary = portions_of(count, rows * top, reach, skew, True), portions_of(count, rows * top, reach, skew, False)
    places = jnp.arange(count)

    def named(tallies, turn):
        used = int((tallies > 0).sum())
        fixed = max(1, used // 4)
        passed = fixed + (places - fixed + turn * (used - fixed)) % max(1, count - fixed)
        return jnp.zeros((count,), jnp.int32).at[order[jnp.where(places < fixed, places, passed)]].set(jnp.asarray(tallies, jnp.int32))

    tallies = jnp.where(number % 4 == 0, named(packed, number // 4), named(ordinary, number - number // 4 - 1))
    mixed = jax.random.permutation(jax.random.fold_in(own, 3), count)
    donor, taker = mixed[0:count // 2 * 2:2], mixed[1:count // 2 * 2:2]
    room = jnp.minimum(tallies[donor] - 1, reach - tallies[taker]) // 2
    room = jnp.where((donor == order[0]) | (taker == order[0]) | (tallies[taker] == 0), 0, jnp.maximum(room, 0))
    passed = jax.random.randint(jax.random.fold_in(own, 4), (count // 2,), 0, 1 << 20) % (room + 1)
    tallies = tallies.at[donor].add(-passed).at[taker].add(passed)
    items = jnp.searchsorted(jnp.cumsum(tallies), jnp.arange(rows * top), side="right").astype(jnp.int32)
    listing = items.reshape(top, rows).T
    listing = listing[jax.random.permutation(jax.random.fold_in(own, 1), rows)]
    turn = jax.random.randint(jax.random.fold_in(own, 2), (rows, 1), 0, top)
    return jnp.take_along_axis(listing, (jnp.arange(top)[None, :] + turn) % top, axis=1)


def portions_of(amount, total, most, slope, full):
    portions = [(1 << 20) // math.isqrt(rank ** slope) + 1 for rank in range(1, amount + 1)]
    largest = most if full else min(most, max(-(-total // amount), total * portions[0] // sum(portions)))
    least = 1 if total - largest >= amount - 1 else 0
    given, surplus = [largest] + [least] * (amount - 1), total - largest - least * (amount - 1)
    while surplus > 0:
        candidates = [i for i in range(1, amount) if given[i] < largest] or [i for i in range(1, amount) if given[i] < most]
        whole, remaining = sum([portions[i] for i in candidates]), surplus
        for i in candidates:
            extra = min(most - given[i], max(1, remaining * portions[i] // whole), surplus)
            given[i] = given[i] + extra
            surplus = surplus - extra
    return np.array(given)


def noise(stream_key, extent, deviation, reach, cuts=(), held_as=jnp.bfloat16):
    factor_of = block_scale(stream_key, extent, cuts, -0.22, 0.18) if cuts else 1.0
    drawn = jax.random.normal(stream_key, extent, jnp.float32) * deviation * factor_of
    return jnp.minimum(jnp.maximum(drawn, -reach), reach).astype(held_as)


def setup_inputs(seed: int = 0) -> dict:
    splits = jax.random.split(jax.random.key(seed), 8)
    images = noise(splits[0], (PARTICLES, BOX * BOX), 1.0, 6.0, ((0, 128), (1, 2)))
    routes_keys = jax.random.split(jax.random.fold_in(splits[1], 1), PARTICLES // PART_DEV)
    routes_turns = jax.random.permutation(jax.random.fold_in(splits[1], 3), PARTICLES // PART_DEV)
    routes = jax.vmap(lambda own, number: shared_out(jax.random.fold_in(splits[1], 2), own, number, PART_DEV, N_POSE, 1, CAP, 2))(routes_keys, routes_turns).reshape((PARTICLES, 1))
    orientations = place_ends(jax.random.randint(splits[2], (PARTICLES,), 0, ORIENT), jax.random.fold_in(splits[2], 1), 0, ORIENT - 1).astype(jnp.int32)
    groups = place_ends(jax.random.randint(splits[3], (PARTICLES,), 0, GROUPS), jax.random.fold_in(splits[3], 1), 0, GROUPS - 1).astype(jnp.int32)
    counts = draw_counts(jax.random.fold_in(splits[7], 71), 0)
    defocus = jnp.clip(jnp.exp(jax.random.uniform(splits[5], (GROUPS,), jnp.float32, math.log(40.0), math.log(160.0))), 40.0, 160.0)
    projections = noise(splits[6], (N_POSE, K, BOX * BOX), (BOX * BOX) ** -0.5, 0.0234375, ((0, 128), (2, 2)))
    return dict(images=images, routes=routes, orientations=orientations, groups=groups, counts=counts, defocus=defocus, projections=projections)


def reference(images, routes, orientations, groups, counts, defocus, projections):
    centre = jnp.arange(BOX).astype(jnp.float32) - jnp.float32(BOX // 2)
    radius = ((centre[:, None] ** 2 + centre[None, :] ** 2) / jnp.float32(BOX * BOX)).reshape(-1)
    ident = jnp.arange(PARTICLES).astype(jnp.int32)
    alive = ident % PART_DEV < counts[ident // PART_DEV]
    target = jnp.where(alive, routes[:, 0], N_POSE).astype(jnp.int32)

    def per_block(block):
        marker = jnp.where(target == block, 0, 1).astype(jnp.int32)
        order = jnp.argsort(marker, stable=True)[:SLOTS].astype(jnp.int32)
        taken = target[order] == block
        ctf = jnp.sin(defocus[groups[order]][:, None] * radius[None, :])
        weighted = (images[order].astype(jnp.float32) * ctf).astype(jnp.bfloat16)
        weighted = jnp.where(taken[:, None], weighted, jnp.zeros_like(weighted))
        scores = jnp.dot(weighted.astype(jnp.float32), projections[block].T.astype(jnp.float32), preferred_element_type=jnp.float32)
        scores = jnp.where(taken[:, None], scores, 0.0)
        onehot = (orientations[order][:, None] == jnp.arange(ORIENT)[None, :]) & taken[:, None]
        weights = (onehot.astype(jnp.float32)[:, :, None] * scores[:, None, :]).reshape(SLOTS, PANEL).astype(jnp.bfloat16)
        panel = jnp.dot(weighted.T.astype(jnp.float32), weights.astype(jnp.float32), preferred_element_type=jnp.float32)
        return (order, scores, panel)
    orders, scores, panels = lax.map(per_block, jnp.arange(N_POSE).astype(jnp.int32))
    coords = jnp.zeros((PARTICLES, K), jnp.float32).at[orders.reshape(-1)].add(scores.reshape(-1, K))
    gram = jnp.einsum('bxp,bxq->pq', panels, panels, precision=lax.Precision.HIGHEST)
    shift = 0.001 * jnp.trace(gram) / PANEL
    lower = jnp.linalg.cholesky(gram + shift * jnp.eye(PANEL, dtype=jnp.float32))
    flat = panels.reshape(N_POSE * BOX * BOX, PANEL)
    solved = lax.linalg.triangular_solve(lower, flat, left_side=False, lower=True, transpose_a=True)
    factor = jnp.sqrt(jnp.float32(N_POSE * BOX * BOX))
    basis = (solved * factor).astype(jnp.bfloat16).reshape(N_POSE, BOX * BOX, PANEL)
    return (coords, basis)
```

```python
import functools

import jax
import jax.numpy as jnp
from jax import lax
from jax.experimental import pallas as pl
from jax.experimental.pallas import tpu as pltpu
from jax.sharding import Mesh, PartitionSpec as P

BOX = 256
K = 16
ORIENT = 4
GROUPS = 8
PANEL = 64
ROWS = 128
NZ = 8
NXY = 16
SLOTS = 256
HALF = 32768
TILE = 4096
SUB = 512
PREFIX = 128
CHUNKS = ((0, 4096), (4096, 8192), (12288, 8192), (20480, 8192), (28672, 4096))
SIZES = (20, 24, 32)

bf16, f32, i32 = jnp.bfloat16, jnp.float32, jnp.int32
HIGH = lax.Precision.HIGHEST
VMEM_LIMIT = 50 * 1024 * 1024


def iota(shape, axis):
    return lax.broadcasted_iota(i32, shape, axis)


def plan_kernel(count_ref, route_ref, orient_ref, group_ref, zkey_ref, place_ref, code_ref, select_ref, most_ref):
    count = count_ref[0]
    first = iota((ROWS, ROWS), 0)
    second = iota((ROWS, ROWS), 1)
    diagonal = first == second

    def column(row):
        return jnp.sum(jnp.where(diagonal, row, 0), axis=1, keepdims=True)

    route = route_ref[...]
    plane, block_xy = route & 7, route >> 3
    route_c = column(route)
    earlier = (first < second) & (first < count)
    rank = jnp.sum(jnp.where(earlier & (route_c == route), 1, 0), axis=0, keepdims=True)
    depth = jnp.sum(jnp.where(earlier & ((route_c & 7) == plane), 1, 0), axis=0, keepdims=True)
    live = iota((1, ROWS), 1) < count
    zkey_ref[...] = jnp.where(live, plane * 32 + depth, -1)
    place_ref[...] = jnp.where(live, route * 2 + rank, -1)
    code = (block_xy * 2 + rank) * ORIENT + orient_ref[...] + 1
    code_ref[...] = jnp.broadcast_to(column(code), (ROWS, ROWS)).astype(f32).astype(bf16)
    select_ref[...] = jnp.where(column(group_ref[...]) == second, 1.0, 0.0)
    most = jnp.max(jnp.where(live, depth + 1, 0), axis=1, keepdims=True)
    most_ref[...] = jnp.broadcast_to(most, (1, ROWS))


def make_plan(routes, orientations, groups, counts):
    vmem = pl.BlockSpec(memory_space=pltpu.VMEM)
    smem = pl.BlockSpec(memory_space=pltpu.SMEM)
    return pl.pallas_call(
        plan_kernel,
        out_shape=(
            jax.ShapeDtypeStruct((1, ROWS), i32),
            jax.ShapeDtypeStruct((1, ROWS), i32),
            jax.ShapeDtypeStruct((ROWS, ROWS), bf16),
            jax.ShapeDtypeStruct((ROWS, ROWS), f32),
            jax.ShapeDtypeStruct((1, ROWS), i32),
        ),
        in_specs=[smem, vmem, vmem, vmem],
        out_specs=(vmem,) * 5,
        cost_estimate=pl.CostEstimate(flops=2**21, bytes_accessed=2**18, transcendentals=0),
        name="plan",
    )(counts, routes.reshape(1, ROWS), orientations.reshape(1, ROWS), groups.reshape(1, ROWS))


def prep_kernel(start, prefix, extra, where_ref, defocus_ref, image_ref, zkey_ref, code_ref, select_ref, *out_refs):
    row_at, z_at = where_ref[0], where_ref[1]
    folds = 16 // extra if extra else 1
    span = TILE // folds
    tile_at = pl.program_id(0) * TILE
    line = iota((ROWS, ROWS), 0)
    target = ((z_at + (line >> 4)) & 7) * 32
    slot = line & 15
    zkey = zkey_ref[...]
    base = (zkey == target + slot)
    stack = [base]
    if extra:
        late = zkey == target + 16 + lax.rem(slot, extra)
        fold_of = lax.div(slot, extra)
    placers = []
    for fold in range(folds):
        parts = [base] + ([late & (fold_of == fold)] if extra else [])
        placers.append(jnp.where(jnp.concatenate(parts, 0), 1.0, 0.0).astype(bf16) if extra else jnp.where(base, 1.0, 0.0).astype(bf16))
    first_pixel = row_at * HALF + start + tile_at
    group = iota((GROUPS, SUB), 0)
    phase = jnp.zeros((GROUPS, SUB), f32)
    for g in range(GROUPS):
        phase = jnp.where(group == g, defocus_ref[g], phase)
    lane = iota((1, SUB), 1)

    def weighted(at):
        pixel = first_pixel + at + lane
        up = ((pixel >> 8) - BOX // 2).astype(f32)
        across = ((pixel & (BOX - 1)) - BOX // 2).astype(f32)
        radius = (up * up + across * across) / f32(BOX * BOX)
        table = jnp.sin(phase * radius)
        ctf = jnp.dot(select_ref[:, :GROUPS], table, precision=HIGH, preferred_element_type=f32)
        return (image_ref[:, at : at + SUB].astype(f32) * ctf).astype(bf16)

    head = PREFIX if prefix else 0
    if prefix:
        codes = code_ref[...]
        front = jnp.dot(placers[0], codes, preferred_element_type=f32).astype(bf16)
        for k in range(NZ):
            block = front[k * 16 : k * 16 + 16]
            if extra:
                block = jnp.where(iota((16, PREFIX), 1) < PREFIX // 2, block, front[ROWS + k * 16 : ROWS + k * 16 + 16])
            out_refs[k][:, 0:PREFIX] = block
    for offset in range(0, span, SUB):
        total = None
        for fold in range(folds):
            at = fold * span + offset
            placed = jnp.dot(placers[fold], weighted(at), preferred_element_type=f32)
            for k in range(NZ):
                out_refs[k][:, head + at : head + at + SUB] = placed[k * 16 : k * 16 + 16].astype(bf16)
            if extra:
                part = placed[ROWS:]
                total = part if total is None else total + part
        if extra:
            for k in range(NZ):
                at = head + TILE + offset
                out_refs[k][:, at : at + SUB] = total[k * 16 : k * 16 + 16].astype(bf16)


def width_of(extra):
    return TILE + TILE * extra // 16


def prep(images, plan, where, defocus, start, size, prefix, extra):
    zkey, code, select = plan
    tiles = size // TILE
    width = width_of(extra) + (PREFIX if prefix else 0)
    assert not prefix or tiles == 1
    smem = pl.BlockSpec(memory_space=pltpu.SMEM)
    whole = lambda shape: pl.BlockSpec(shape, lambda t: (0, 0))
    return pl.pallas_call(
        functools.partial(prep_kernel, start, prefix, extra),
        out_shape=(jax.ShapeDtypeStruct((16, tiles * width), bf16),) * NZ,
        grid=(tiles,),
        in_specs=[
            smem,
            smem,
            pl.BlockSpec((ROWS, TILE), lambda t: (0, start // TILE + t)),
            whole((1, ROWS)),
            whole((ROWS, ROWS)),
            whole((ROWS, ROWS)),
        ],
        out_specs=(pl.BlockSpec((16, width), lambda t: (0, t)),) * NZ,
        compiler_params=pltpu.CompilerParams(vmem_limit_bytes=VMEM_LIMIT),
        cost_estimate=pl.CostEstimate(flops=tiles * 2**28, bytes_accessed=tiles * 2**21, transcendentals=0),
        name="prep",
    )(where, defocus, images, zkey, code, select)


def spread_kernel(prefix, extra, *refs):
    folds = 16 // extra if extra else 1
    span = TILE // folds
    head = PREFIX if prefix else 0
    if prefix:
        where_ref, piece_refs, (out_ref, placer_ref) = refs[0], refs[1 : 1 + NZ], refs[2 + NZ :]
        z_at = where_ref[1]
        codes = jnp.concatenate([ref[:, 0:PREFIX] for ref in piece_refs], 0).astype(f32)
        line = iota((ROWS, SLOTS), 0)
        owner_slot = iota((ROWS, SLOTS), 1)
        source_z = (z_at - (line >> 4)) & 7
        halves = []
        for half in range(2 if extra else 1):
            code = codes[:, half * (PREFIX // 2) : half * (PREFIX // 2) + 1].astype(i32)
            if half:
                filled = (code > 0) & ((iota((ROWS, 1), 0) & 15) < extra)
            else:
                filled = code > 0
            ticket = code - 1
            slot = (ticket >> 3) * 16 + source_z * 2 + ((ticket >> 2) & 1)
            hit = filled & (slot == owner_slot)
            halves.append(jnp.where(hit, 1.0, 0.0).T)
        placer = jnp.concatenate(halves, 1) if extra else halves[0]
        placer_ref[...] = placer.astype(bf16)
    else:
        placer_in, piece_refs, (out_ref,) = refs[0], refs[1 : 1 + NZ], refs[2 + NZ :]
        placer = placer_in[...].astype(f32)
    base = placer[:, :ROWS].astype(bf16)
    if prefix:
        lanes = iota((ROWS, PREFIX), 1)
        early = jnp.concatenate([ref[:, 0:PREFIX] for ref in piece_refs], 0).astype(f32)
        front = jnp.dot(base, jnp.broadcast_to(early[:, 0:1], (ROWS, PREFIX)).astype(bf16), preferred_element_type=f32)
        if extra:
            late = placer[:, ROWS:].astype(bf16)
            later = jnp.broadcast_to(early[:, PREFIX // 2 : PREFIX // 2 + 1], (ROWS, PREFIX)).astype(bf16)
            front = front + jnp.dot(late, later, preferred_element_type=f32)
        out_ref[:, :, 0:PREFIX] = front.astype(bf16).reshape(NXY, 16, PREFIX)
    spread = []
    if extra:
        late = placer[:, ROWS:]
        column = iota((ROWS, ROWS), 1)
        row = iota((ROWS, ROWS), 0)
        for fold in range(folds):
            move = (column == (row & ~15) + fold * extra + (row & 15)) & ((row & 15) < extra)
            spread.append(jnp.dot(late.astype(bf16), jnp.where(move, 1.0, 0.0).astype(bf16), preferred_element_type=f32).astype(bf16))
    for fold in range(folds):
        for offset in range(0, span, SUB):
            at = fold * span + offset
            piece = jnp.concatenate([ref[:, head + at : head + at + SUB] for ref in piece_refs], 0)
            out = jnp.dot(base, piece, preferred_element_type=f32)
            if extra:
                lat = head + TILE + offset
                piece = jnp.concatenate([ref[:, lat : lat + SUB] for ref in piece_refs], 0)
                out = out + jnp.dot(spread[fold], piece, preferred_element_type=f32)
            out_ref[:, :, head + at : head + at + SUB] = out.astype(bf16).reshape(NXY, 16, SUB)


def spread(pieces, control, after, size, prefix, extra):
    tiles = size // TILE
    head = PREFIX if prefix else 0
    width = width_of(extra) + head
    columns = ROWS * 2 if extra else ROWS
    out_shape = jax.ShapeDtypeStruct((NXY, 16, size + head), bf16)
    out_spec = pl.BlockSpec((NXY, 16, TILE + head), lambda t: (0, 0, t))
    placer_spec = pl.BlockSpec((SLOTS, columns), lambda t: (0, 0))
    return pl.pallas_call(
        functools.partial(spread_kernel, prefix, extra),
        out_shape=(out_shape, jax.ShapeDtypeStruct((SLOTS, columns), bf16)) if prefix else out_shape,
        grid=(tiles,),
        in_specs=[pl.BlockSpec(memory_space=pltpu.SMEM) if prefix else placer_spec]
        + [pl.BlockSpec((16, width), lambda t: (0, t))] * NZ
        + [pl.BlockSpec(memory_space=pl.ANY)],
        out_specs=(out_spec, placer_spec) if prefix else out_spec,
        compiler_params=pltpu.CompilerParams(vmem_limit_bytes=VMEM_LIMIT),
        cost_estimate=pl.CostEstimate(flops=tiles * 2**29, bytes_accessed=tiles * 2**22, transcendentals=0),
        name="spread",
    )(control, *pieces, after)


def products_kernel(head, rows_ref, project_ref, gram_in, score_in, gram_ref, score_ref):
    @pl.when(pl.program_id(0) == 0)
    def _():
        gram_ref[...] = gram_in[...]
        score_ref[...] = score_in[...]

    rows = rows_ref[:, head:]
    contract = (((1,), (1,)), ((), ()))
    gram_ref[...] += lax.dot_general(rows, rows, contract, preferred_element_type=f32)
    score_ref[...] += lax.dot_general(rows, project_ref[...], contract, preferred_element_type=f32)


def products(rows, project, gram, score, start, size, prefix):
    tiles = size // TILE
    head = PREFIX if prefix else 0
    whole = lambda shape: pl.BlockSpec(shape, lambda t: (0, 0))
    return pl.pallas_call(
        functools.partial(products_kernel, head),
        out_shape=(jax.ShapeDtypeStruct((SLOTS, SLOTS), f32), jax.ShapeDtypeStruct((SLOTS, K), f32)),
        grid=(tiles,),
        in_specs=[
            pl.BlockSpec((SLOTS, TILE + head), lambda t: (0, t)),
            pl.BlockSpec((K, TILE), lambda t: (0, start // TILE + t)),
            whole((SLOTS, SLOTS)),
            whole((SLOTS, K)),
        ],
        out_specs=(whole((SLOTS, SLOTS)), whole((SLOTS, K))),
        compiler_params=pltpu.CompilerParams(vmem_limit_bytes=VMEM_LIMIT),
        cost_estimate=pl.CostEstimate(flops=tiles * 2**29, bytes_accessed=tiles * 2**21, transcendentals=0),
        name="products",
    )(rows, project, gram, score)


def weights_of(score, code):
    ticket = code - 1
    orient = ticket & 3
    tiled = jnp.concatenate([score] * ORIENT, axis=1)
    panel_o = iota((SLOTS, PANEL), 1) >> 4
    return jnp.where((ticket >= 0) & (panel_o == orient), tiled, 0.0).astype(bf16)


def local_gram_kernel(score_ref, other_ref, front_ref, gram_ref, total_ref, weight_ref, local_ref):
    score = score_ref[...] + other_ref[...]
    total_ref[...] = score
    code = front_ref[:, 0:1].astype(f32).astype(i32)
    weight = weights_of(score, code)
    weight_ref[...] = weight
    wide = weight.astype(f32)
    middle = jnp.dot(gram_ref[...], wide, precision=HIGH, preferred_element_type=f32)
    local_ref[...] = lax.dot_general(wide, middle, (((0,), (0,)), ((), ())), precision=HIGH, preferred_element_type=f32)


def local_gram(score, other, first_rows, gram):
    whole = lambda shape: pl.BlockSpec(shape, lambda: (0, 0))
    return pl.pallas_call(
        local_gram_kernel,
        out_shape=(
            jax.ShapeDtypeStruct((SLOTS, K), f32),
            jax.ShapeDtypeStruct((SLOTS, PANEL), bf16),
            jax.ShapeDtypeStruct((PANEL, PANEL), f32),
        ),
        in_specs=[whole((SLOTS, K)), whole((SLOTS, K)), whole((SLOTS, PREFIX)), whole((SLOTS, SLOTS))],
        out_specs=(whole((SLOTS, K)), whole((SLOTS, PANEL)), whole((PANEL, PANEL))),
        compiler_params=pltpu.CompilerParams(vmem_limit_bytes=VMEM_LIMIT),
        cost_estimate=pl.CostEstimate(flops=2**27, bytes_accessed=2**19, transcendentals=0),
        name="local_gram",
    )(score, other, first_rows, gram)


def factor_kernel(gram_ref, weight_ref, mix_ref):
    gram = gram_ref[...]
    first = iota((PANEL, PANEL), 0)
    second = iota((PANEL, PANEL), 1)
    same = jnp.where(first == second, 1.0, 0.0)
    shift = 0.001 * jnp.sum(gram * same) / PANEL
    wide = jnp.concatenate([gram + shift * same, same], axis=1)
    line = iota((PANEL, 2 * PANEL), 0)
    lane = iota((1, 2 * PANEL), 1)
    for j in range(PANEL):
        row = wide[j : j + 1, :]
        pivot = wide[j : j + 1, j : j + 1]
        scaled = row * lax.rsqrt(pivot)
        inverse = 1.0 / pivot
        column = wide[:, j : j + 1] * inverse
        below = line > j
        wide = jnp.where(below, wide - column * row, jnp.where(line == j, scaled, wide))
    inverse_lower = wide[:, PANEL:]
    mix = lax.dot_general(
        inverse_lower, weight_ref[...].astype(f32), (((1,), (1,)), ((), ())), precision=HIGH, preferred_element_type=f32
    ) * f32(float(128 * BOX * BOX) ** 0.5)
    high = mix.astype(bf16)
    low = (mix - high.astype(f32)).astype(bf16)
    mix_ref[...] = jnp.concatenate([high, low], axis=0)


def factor(gram, weight):
    whole = lambda shape: pl.BlockSpec(shape, lambda: (0, 0))
    return pl.pallas_call(
        factor_kernel,
        out_shape=jax.ShapeDtypeStruct((2 * PANEL, SLOTS), bf16),
        in_specs=[whole((PANEL, PANEL)), whole((SLOTS, PANEL))],
        out_specs=whole((2 * PANEL, SLOTS)),
        cost_estimate=pl.CostEstimate(flops=2**23, bytes_accessed=2**17, transcendentals=0),
        name="factor",
    )(gram, weight)


def basis_kernel(mix_ref, *refs):
    row_refs, out_ref = refs[:-1], refs[-1]
    step = pl.program_id(0)
    mix = mix_ref[...]
    for (start, size), ref in zip(CHUNKS, row_refs):
        head = PREFIX if start == 0 else 0

        @pl.when((step >= start // TILE) & (step < (start + size) // TILE))
        def _(ref=ref, head=head):
            both = jnp.dot(mix, ref[:, head:], preferred_element_type=f32)
            out_ref[...] = (both[:PANEL] + both[PANEL:]).astype(bf16)


def make_basis(mix, chunks):
    specs = []
    for start, size in CHUNKS:
        head = PREFIX if start == 0 else 0
        first, count = start // TILE, size // TILE
        specs.append(pl.BlockSpec((SLOTS, TILE + head), lambda t, first=first, count=count: (0, jnp.clip(t - first, 0, count - 1))))
    return pl.pallas_call(
        basis_kernel,
        out_shape=jax.ShapeDtypeStruct((PANEL, HALF), bf16),
        grid=(HALF // TILE,),
        in_specs=[pl.BlockSpec((2 * PANEL, SLOTS), lambda t: (0, 0))] + specs,
        out_specs=pl.BlockSpec((PANEL, TILE), lambda t: (0, t)),
        compiler_params=pltpu.CompilerParams(vmem_limit_bytes=VMEM_LIMIT),
        cost_estimate=pl.CostEstimate(flops=2**31, bytes_accessed=2**24, transcendentals=0),
        name="basis",
    )(mix, *chunks)


def shift_z(block, k):
    if k == 0:
        return block
    return lax.ppermute(block, "z", [(i, (i + k) % NZ) for i in range(NZ)])


def swap_row(value):
    return lax.ppermute(value, "row", [(0, 1), (1, 0)])


def sum_everywhere(value):
    value = value + swap_row(value)
    for axis, size in (("z", 8), ("x", 4), ("y", 4)):
        step = 1
        while step < size:
            value = value + lax.ppermute(value, axis, [(i, i ^ step) for i in range(size)])
            step *= 2
    return value


def most_everywhere(value):
    for axis, size in (("z", 8), ("x", 4), ("y", 4)):
        step = 1
        while step < size:
            value = jnp.maximum(value, lax.ppermute(value, axis, [(i, i ^ step) for i in range(size)]))
            step *= 2
    return value


def exchange(size, images, project, plan, where, defocus):
    extra = size - 16
    gram = jnp.zeros((SLOTS, SLOTS), f32)
    score = jnp.zeros((SLOTS, K), f32)
    arrived = []
    control = where
    made = [prep(images, plan, where, defocus, start, length, start == 0, extra) for start, length in CHUNKS]
    for at, (start, length) in enumerate(CHUNKS):
        prefix = start == 0
        pieces = [None] * NZ
        for k in (0, 1, 7, 2, 6, 3, 5, 4):
            pieces[k] = shift_z(made[at][k], k)
        after = made[min(at + 1, len(CHUNKS) - 1)][0]
        out = spread(pieces, control, after, length, prefix, extra)
        if prefix:
            out, control = out
        rows = lax.all_to_all(out, ("x", "y"), 0, 0, tiled=True).reshape(SLOTS, -1)
        gram, score = products(rows, project, gram, score, start, length, prefix)
        arrived.append(rows)
    return gram, score, tuple(arrived)


def shards(images, routes, orientations, groups, counts, defocus, projections):
    project = projections[0]
    where = jnp.stack([lax.axis_index("row"), lax.axis_index("z")]).astype(i32)
    zkey, place, code, select, most = make_plan(routes, orientations, groups, counts)
    plan = (zkey, code, select)
    operands = (images, project, plan, where, defocus)
    if len(SIZES) == 1:
        gram, score, arrived = exchange(SIZES[0], *operands)
    else:
        top = most_everywhere(most)[0, 0]
        index = sum((top > size).astype(i32) for size in SIZES[:-1])
        gram, score, arrived = lax.switch(index, [functools.partial(exchange, size) for size in SIZES], *operands)
    front = arrived[0][:, :PREFIX]
    score, weight, local = local_gram(score, swap_row(score), front, gram)
    returned = lax.all_to_all(score.reshape(128, 2, K), ("x", "y", "z"), 0, 0, tiled=True).reshape(SLOTS, K)
    placer = (place.reshape(ROWS, 1) == jnp.arange(SLOTS)[None, :]).astype(f32)
    coords = jnp.dot(placer, returned, precision=HIGH)
    total = sum_everywhere(local)
    basis = make_basis(factor(total, weight), arrived)
    return coords, basis.T.reshape(1, HALF, PANEL)


def solution(mesh):
    split = Mesh(mesh.devices.reshape(4, 4, 8, 2), ("x", "y", "z", "row"))
    pose = ("x", "y", "z")
    in_specs = (P(pose, "row"), P(pose, None), P(pose), P(pose), P(pose), P(), P(pose, None, "row"))
    out_specs = (P(pose, None), P(pose, "row", None))
    return jax.shard_map(shards, mesh=split, in_specs=in_specs, out_specs=out_specs, check_vma=False)
```

```python
import functools

import jax
import jax.numpy as jnp
from jax import lax
from jax.experimental import pallas as pl
from jax.experimental.pallas import tpu as pltpu
from jax.sharding import Mesh, PartitionSpec as P

BOX = 256
K = 16
ORIENT = 4
GROUPS = 8
PANEL = 64
ROWS = 128
NZ = 8
NXY = 16
SLOTS = 256
HALF = 32768
TILE = 4096
SUB = 512
PREFIX = 128
CHUNKS = ((0, 4096), (4096, 8192), (12288, 8192), (20480, 4096), (24576, 4096), (28672, 4096))
SIZES = (20, 24, 32)

bf16, f32, i32 = jnp.bfloat16, jnp.float32, jnp.int32
HIGH = lax.Precision.HIGHEST
VMEM_LIMIT = 50 * 1024 * 1024


def iota(shape, axis):
    return lax.broadcasted_iota(i32, shape, axis)


def plan_kernel(count_ref, route_ref, orient_ref, group_ref, zkey_ref, place_ref, code_ref, select_ref, most_ref):
    count = count_ref[0]
    first = iota((ROWS, ROWS), 0)
    second = iota((ROWS, ROWS), 1)
    diagonal = first == second

    def column(row):
        return jnp.sum(jnp.where(diagonal, row, 0), axis=1, keepdims=True)

    route = route_ref[...]
    plane, block_xy = route & 7, route >> 3
    route_c = column(route)
    earlier = (first < second) & (first < count)
    rank = jnp.sum(jnp.where(earlier & (route_c == route), 1, 0), axis=0, keepdims=True)
    depth = jnp.sum(jnp.where(earlier & ((route_c & 7) == plane), 1, 0), axis=0, keepdims=True)
    live = iota((1, ROWS), 1) < count
    zkey_ref[...] = jnp.where(live, plane * 32 + depth, -1)
    place_ref[...] = jnp.where(live, route * 2 + rank, -1)
    code = (block_xy * 2 + rank) * ORIENT + orient_ref[...] + 1
    code_ref[...] = jnp.broadcast_to(column(code), (ROWS, ROWS)).astype(f32).astype(bf16)
    select_ref[...] = jnp.where(column(group_ref[...]) == second, 1.0, 0.0)
    most = jnp.max(jnp.where(live, depth + 1, 0), axis=1, keepdims=True)
    most_ref[...] = jnp.broadcast_to(most, (1, ROWS))


def make_plan(routes, orientations, groups, counts):
    vmem = pl.BlockSpec(memory_space=pltpu.VMEM)
    smem = pl.BlockSpec(memory_space=pltpu.SMEM)
    return pl.pallas_call(
        plan_kernel,
        out_shape=(
            jax.ShapeDtypeStruct((1, ROWS), i32),
            jax.ShapeDtypeStruct((1, ROWS), i32),
            jax.ShapeDtypeStruct((ROWS, ROWS), bf16),
            jax.ShapeDtypeStruct((ROWS, ROWS), f32),
            jax.ShapeDtypeStruct((1, ROWS), i32),
        ),
        in_specs=[smem, vmem, vmem, vmem],
        out_specs=(vmem,) * 5,
        cost_estimate=pl.CostEstimate(flops=2**21, bytes_accessed=2**18, transcendentals=0),
        name="plan",
    )(counts, routes.reshape(1, ROWS), orientations.reshape(1, ROWS), groups.reshape(1, ROWS))


def prep_kernel(start, prefix, extra, where_ref, defocus_ref, image_ref, zkey_ref, code_ref, select_ref, *refs):
    out_refs = refs[-NZ:]
    row_at, z_at = where_ref[0], where_ref[1]
    folds = 16 // extra if extra else 1
    span = TILE // folds
    tile_at = pl.program_id(0) * TILE
    line = iota((ROWS, ROWS), 0)
    target = ((z_at + (line >> 4)) & 7) * 32
    slot = line & 15
    zkey = zkey_ref[...]
    base = (zkey == target + slot)
    stack = [base]
    if extra:
        late = zkey == target + 16 + lax.rem(slot, extra)
        fold_of = lax.div(slot, extra)
    placers = []
    for fold in range(folds):
        parts = [base] + ([late & (fold_of == fold)] if extra else [])
        placers.append(jnp.where(jnp.concatenate(parts, 0), 1.0, 0.0).astype(bf16) if extra else jnp.where(base, 1.0, 0.0).astype(bf16))
    first_pixel = row_at * HALF + start + tile_at
    group = iota((GROUPS, SUB), 0)
    phase = jnp.zeros((GROUPS, SUB), f32)
    for g in range(GROUPS):
        phase = jnp.where(group == g, defocus_ref[g], phase)
    lane = iota((1, SUB), 1)

    def weighted(at):
        pixel = first_pixel + at + lane
        up = ((pixel >> 8) - BOX // 2).astype(f32)
        across = ((pixel & (BOX - 1)) - BOX // 2).astype(f32)
        radius = (up * up + across * across) / f32(BOX * BOX)
        table = jnp.sin(phase * radius)
        ctf = jnp.dot(select_ref[:, :GROUPS], table, precision=HIGH, preferred_element_type=f32)
        return (image_ref[:, at : at + SUB].astype(f32) * ctf).astype(bf16)

    head = PREFIX if prefix else 0
    if prefix:
        codes = code_ref[...]
        front = jnp.dot(placers[0], codes, preferred_element_type=f32).astype(bf16)
        for k in range(NZ):
            block = front[k * 16 : k * 16 + 16]
            if extra:
                block = jnp.where(iota((16, PREFIX), 1) < PREFIX // 2, block, front[ROWS + k * 16 : ROWS + k * 16 + 16])
            out_refs[k][:, 0:PREFIX] = block
    for offset in range(0, span, SUB):
        total = None
        for fold in range(folds):
            at = fold * span + offset
            placed = jnp.dot(placers[fold], weighted(at), preferred_element_type=f32)
            for k in range(NZ):
                out_refs[k][:, head + at : head + at + SUB] = placed[k * 16 : k * 16 + 16].astype(bf16)
            if extra:
                part = placed[ROWS:]
                total = part if total is None else total + part
        if extra:
            for k in range(NZ):
                at = head + TILE + offset
                out_refs[k][:, at : at + SUB] = total[k * 16 : k * 16 + 16].astype(bf16)


def width_of(extra):
    return TILE + TILE * extra // 16


def prep(images, plan, where, defocus, after, start, size, prefix, extra):
    zkey, code, select = plan
    tiles = size // TILE
    width = width_of(extra) + (PREFIX if prefix else 0)
    assert not prefix or tiles == 1
    smem = pl.BlockSpec(memory_space=pltpu.SMEM)
    whole = lambda shape: pl.BlockSpec(shape, lambda t: (0, 0))
    return pl.pallas_call(
        functools.partial(prep_kernel, start, prefix, extra),
        out_shape=(jax.ShapeDtypeStruct((16, tiles * width), bf16),) * NZ,
        grid=(tiles,),
        in_specs=[
            smem,
            smem,
            pl.BlockSpec((ROWS, TILE), lambda t: (0, start // TILE + t)),
            whole((1, ROWS)),
            whole((ROWS, ROWS)),
            whole((ROWS, ROWS)),
        ]
        + [pl.BlockSpec(memory_space=pl.ANY)] * len(after),
        out_specs=(pl.BlockSpec((16, width), lambda t: (0, t)),) * NZ,
        compiler_params=pltpu.CompilerParams(vmem_limit_bytes=VMEM_LIMIT),
        cost_estimate=pl.CostEstimate(flops=2**36, bytes_accessed=tiles * 2**21, transcendentals=0),
        name="prep",
    )(where, defocus, images, zkey, code, select, *after)


def spread_kernel(prefix, extra, *refs):
    folds = 16 // extra if extra else 1
    span = TILE // folds
    head = PREFIX if prefix else 0
    if prefix:
        where_ref, piece_refs, (out_ref, placer_ref) = refs[0], refs[1 : 1 + NZ], refs[-2:]
        z_at = where_ref[1]
        codes = jnp.concatenate([ref[:, 0:PREFIX] for ref in piece_refs], 0).astype(f32)
        line = iota((ROWS, SLOTS), 0)
        owner_slot = iota((ROWS, SLOTS), 1)
        source_z = (z_at - (line >> 4)) & 7
        halves = []
        for half in range(2 if extra else 1):
            code = codes[:, half * (PREFIX // 2) : half * (PREFIX // 2) + 1].astype(i32)
            if half:
                filled = (code > 0) & ((iota((ROWS, 1), 0) & 15) < extra)
            else:
                filled = code > 0
            ticket = code - 1
            slot = (ticket >> 3) * 16 + source_z * 2 + ((ticket >> 2) & 1)
            hit = filled & (slot == owner_slot)
            halves.append(jnp.where(hit, 1.0, 0.0).T)
        placer = jnp.concatenate(halves, 1) if extra else halves[0]
        placer_ref[...] = placer.astype(bf16)
    else:
        placer_in, piece_refs, out_ref = refs[0], refs[1 : 1 + NZ], refs[-1]
        placer = placer_in[...].astype(f32)
    base = placer[:, :ROWS].astype(bf16)
    if prefix:
        lanes = iota((ROWS, PREFIX), 1)
        early = jnp.concatenate([ref[:, 0:PREFIX] for ref in piece_refs], 0).astype(f32)
        front = jnp.dot(base, jnp.broadcast_to(early[:, 0:1], (ROWS, PREFIX)).astype(bf16), preferred_element_type=f32)
        if extra:
            late = placer[:, ROWS:].astype(bf16)
            later = jnp.broadcast_to(early[:, PREFIX // 2 : PREFIX // 2 + 1], (ROWS, PREFIX)).astype(bf16)
            front = front + jnp.dot(late, later, preferred_element_type=f32)
        out_ref[:, :, 0:PREFIX] = front.astype(bf16).reshape(NXY, 16, PREFIX)
    spread = []
    if extra:
        late = placer[:, ROWS:]
        column = iota((ROWS, ROWS), 1)
        row = iota((ROWS, ROWS), 0)
        for fold in range(folds):
            move = (column == (row & ~15) + fold * extra + (row & 15)) & ((row & 15) < extra)
            spread.append(jnp.dot(late.astype(bf16), jnp.where(move, 1.0, 0.0).astype(bf16), preferred_element_type=f32).astype(bf16))
    for fold in range(folds):
        for offset in range(0, span, SUB):
            at = fold * span + offset
            piece = jnp.concatenate([ref[:, head + at : head + at + SUB] for ref in piece_refs], 0)
            out = jnp.dot(base, piece, preferred_element_type=f32)
            if extra:
                lat = head + TILE + offset
                piece = jnp.concatenate([ref[:, lat : lat + SUB] for ref in piece_refs], 0)
                out = out + jnp.dot(spread[fold], piece, preferred_element_type=f32)
            out_ref[:, :, head + at : head + at + SUB] = out.astype(bf16).reshape(NXY, 16, SUB)


def spread(pieces, control, after, size, prefix, extra):
    tiles = size // TILE
    head = PREFIX if prefix else 0
    width = width_of(extra) + head
    columns = ROWS * 2 if extra else ROWS
    out_shape = jax.ShapeDtypeStruct((NXY, 16, size + head), bf16)
    out_spec = pl.BlockSpec((NXY, 16, TILE + head), lambda t: (0, 0, t))
    placer_spec = pl.BlockSpec((SLOTS, columns), lambda t: (0, 0))
    return pl.pallas_call(
        functools.partial(spread_kernel, prefix, extra),
        out_shape=(out_shape, jax.ShapeDtypeStruct((SLOTS, columns), bf16)) if prefix else out_shape,
        grid=(tiles,),
        in_specs=[pl.BlockSpec(memory_space=pltpu.SMEM) if prefix else placer_spec]
        + [pl.BlockSpec((16, width), lambda t: (0, t))] * NZ
        + [pl.BlockSpec(memory_space=pl.ANY)] * len(after),
        out_specs=(out_spec, placer_spec) if prefix else out_spec,
        compiler_params=pltpu.CompilerParams(vmem_limit_bytes=VMEM_LIMIT),
        cost_estimate=pl.CostEstimate(flops=2**36, bytes_accessed=tiles * 2**22, transcendentals=0),
        name="spread",
    )(control, *pieces, *after)


def products_kernel(head, rows_ref, project_ref, gram_in, score_in, gram_ref, score_ref):
    @pl.when(pl.program_id(0) == 0)
    def _():
        gram_ref[...] = gram_in[...]
        score_ref[...] = score_in[...]

    rows = rows_ref[:, head:]
    contract = (((1,), (1,)), ((), ()))
    gram_ref[...] += lax.dot_general(rows, rows, contract, preferred_element_type=f32)
    score_ref[...] += lax.dot_general(rows, project_ref[...], contract, preferred_element_type=f32)


def products(rows, project, gram, score, start, size, prefix):
    tiles = size // TILE
    head = PREFIX if prefix else 0
    whole = lambda shape: pl.BlockSpec(shape, lambda t: (0, 0))
    return pl.pallas_call(
        functools.partial(products_kernel, head),
        out_shape=(jax.ShapeDtypeStruct((SLOTS, SLOTS), f32), jax.ShapeDtypeStruct((SLOTS, K), f32)),
        grid=(tiles,),
        in_specs=[
            pl.BlockSpec((SLOTS, TILE + head), lambda t: (0, t)),
            pl.BlockSpec((K, TILE), lambda t: (0, start // TILE + t)),
            whole((SLOTS, SLOTS)),
            whole((SLOTS, K)),
        ],
        out_specs=(whole((SLOTS, SLOTS)), whole((SLOTS, K))),
        compiler_params=pltpu.CompilerParams(vmem_limit_bytes=VMEM_LIMIT),
        cost_estimate=pl.CostEstimate(flops=2**36, bytes_accessed=tiles * 2**21, transcendentals=0),
        name="products",
    )(rows, project, gram, score)


def weights_of(score, code):
    ticket = code - 1
    orient = ticket & 3
    tiled = jnp.concatenate([score] * ORIENT, axis=1)
    panel_o = iota((SLOTS, PANEL), 1) >> 4
    return jnp.where((ticket >= 0) & (panel_o == orient), tiled, 0.0).astype(bf16)


def local_gram_kernel(score_ref, other_ref, front_ref, gram_ref, total_ref, weight_ref, local_ref):
    score = score_ref[...] + other_ref[...]
    total_ref[...] = score
    code = front_ref[:, 0:1].astype(f32).astype(i32)
    weight = weights_of(score, code)
    weight_ref[...] = weight
    wide = weight.astype(f32)
    middle = jnp.dot(gram_ref[...], wide, precision=HIGH, preferred_element_type=f32)
    local_ref[...] = lax.dot_general(wide, middle, (((0,), (0,)), ((), ())), precision=HIGH, preferred_element_type=f32)


def local_gram(score, other, first_rows, gram):
    whole = lambda shape: pl.BlockSpec(shape, lambda: (0, 0))
    return pl.pallas_call(
        local_gram_kernel,
        out_shape=(
            jax.ShapeDtypeStruct((SLOTS, K), f32),
            jax.ShapeDtypeStruct((SLOTS, PANEL), bf16),
            jax.ShapeDtypeStruct((PANEL, PANEL), f32),
        ),
        in_specs=[whole((SLOTS, K)), whole((SLOTS, K)), whole((SLOTS, PREFIX)), whole((SLOTS, SLOTS))],
        out_specs=(whole((SLOTS, K)), whole((SLOTS, PANEL)), whole((PANEL, PANEL))),
        compiler_params=pltpu.CompilerParams(vmem_limit_bytes=VMEM_LIMIT),
        cost_estimate=pl.CostEstimate(flops=2**27, bytes_accessed=2**19, transcendentals=0),
        name="local_gram",
    )(score, other, first_rows, gram)


def factor_kernel(gram_ref, weight_ref, mix_ref):
    gram = gram_ref[...]
    first = iota((PANEL, PANEL), 0)
    second = iota((PANEL, PANEL), 1)
    same = jnp.where(first == second, 1.0, 0.0)
    shift = 0.001 * jnp.sum(gram * same) / PANEL
    wide = jnp.concatenate([gram + shift * same, same], axis=1)
    line = iota((PANEL, 2 * PANEL), 0)
    lane = iota((1, 2 * PANEL), 1)
    for j in range(PANEL):
        row = wide[j : j + 1, :]
        pivot = wide[j : j + 1, j : j + 1]
        scaled = row * lax.rsqrt(pivot)
        inverse = 1.0 / pivot
        column = wide[:, j : j + 1] * inverse
        below = line > j
        wide = jnp.where(below, wide - column * row, jnp.where(line == j, scaled, wide))
    inverse_lower = wide[:, PANEL:]
    mix = lax.dot_general(
        inverse_lower, weight_ref[...].astype(f32), (((1,), (1,)), ((), ())), precision=HIGH, preferred_element_type=f32
    ) * f32(float(128 * BOX * BOX) ** 0.5)
    high = mix.astype(bf16)
    low = (mix - high.astype(f32)).astype(bf16)
    mix_ref[...] = jnp.concatenate([high, low], axis=0)


def factor(gram, weight):
    whole = lambda shape: pl.BlockSpec(shape, lambda: (0, 0))
    return pl.pallas_call(
        factor_kernel,
        out_shape=jax.ShapeDtypeStruct((2 * PANEL, SLOTS), bf16),
        in_specs=[whole((PANEL, PANEL)), whole((SLOTS, PANEL))],
        out_specs=whole((2 * PANEL, SLOTS)),
        cost_estimate=pl.CostEstimate(flops=2**23, bytes_accessed=2**17, transcendentals=0),
        name="factor",
    )(gram, weight)


def basis_kernel(mix_ref, *refs):
    row_refs, out_ref = refs[:-1], refs[-1]
    step = pl.program_id(0)
    mix = mix_ref[...]
    for (start, size), ref in zip(CHUNKS, row_refs):
        head = PREFIX if start == 0 else 0

        @pl.when((step >= start // TILE) & (step < (start + size) // TILE))
        def _(ref=ref, head=head):
            both = jnp.dot(mix, ref[:, head:], preferred_element_type=f32)
            out_ref[...] = (both[:PANEL] + both[PANEL:]).astype(bf16)


def make_basis(mix, chunks):
    specs = []
    for start, size in CHUNKS:
        head = PREFIX if start == 0 else 0
        first, count = start // TILE, size // TILE
        specs.append(pl.BlockSpec((SLOTS, TILE + head), lambda t, first=first, count=count: (0, jnp.clip(t - first, 0, count - 1))))
    return pl.pallas_call(
        basis_kernel,
        out_shape=jax.ShapeDtypeStruct((PANEL, HALF), bf16),
        grid=(HALF // TILE,),
        in_specs=[pl.BlockSpec((2 * PANEL, SLOTS), lambda t: (0, 0))] + specs,
        out_specs=pl.BlockSpec((PANEL, TILE), lambda t: (0, t)),
        compiler_params=pltpu.CompilerParams(vmem_limit_bytes=VMEM_LIMIT),
        cost_estimate=pl.CostEstimate(flops=2**31, bytes_accessed=2**24, transcendentals=0),
        name="basis",
    )(mix, *chunks)


def shift_z(block, k):
    if k == 0:
        return block
    return lax.ppermute(block, "z", [(i, (i + k) % NZ) for i in range(NZ)])


def swap_row(value):
    return lax.ppermute(value, "row", [(0, 1), (1, 0)])


def sum_everywhere(value):
    value = value + swap_row(value)
    for axis, size in (("z", 8), ("x", 4), ("y", 4)):
        step = 1
        while step < size:
            value = value + lax.ppermute(value, axis, [(i, i ^ step) for i in range(size)])
            step *= 2
    return value


def most_everywhere(value):
    for axis, size in (("z", 8), ("x", 4), ("y", 4)):
        step = 1
        while step < size:
            value = jnp.maximum(value, lax.ppermute(value, axis, [(i, i ^ step) for i in range(size)]))
            step *= 2
    return value


def finish(gram, score, arrived, place):
    front = arrived[0][:, :PREFIX]
    score, weight, local = local_gram(score, swap_row(score), front, gram)
    returned = lax.all_to_all(score.reshape(128, 2, K), ("x", "y", "z"), 0, 0, tiled=True).reshape(SLOTS, K)
    placer = (place.reshape(ROWS, 1) == jnp.arange(SLOTS)[None, :]).astype(f32)
    coords = jnp.dot(placer, returned, precision=HIGH)
    total = sum_everywhere(local)
    basis = make_basis(factor(total, weight), arrived)
    return coords, basis.T.reshape(1, HALF, PANEL)


def exchange(size, images, project, plan, place, where, defocus):
    extra = size - 16
    gram = jnp.zeros((SLOTS, SLOTS), f32)
    score = jnp.zeros((SLOTS, K), f32)
    arrived, grams = [], []
    control = where
    made = {}
    outs = {}

    def make(at):
        if at < len(CHUNKS):
            start, length = CHUNKS[at]
            after = [outs[at - 2]] if at >= 2 else []
            made[at] = prep(images, plan, where, defocus, after, start, length, start == 0, extra)

    make(0)
    make(1)
    for at, (start, length) in enumerate(CHUNKS):
        prefix = start == 0
        pieces = [shift_z(made[at][k], k) for k in range(NZ)]
        after = [made[at + 1][0]] if at + 1 < len(CHUNKS) else []
        after += arrived[-1:] + ([grams[at - 2]] if at >= 2 else [])
        out = spread(pieces, control, after, length, prefix, extra)
        if prefix:
            out, control = out
        outs[at] = out
        make(at + 2)
        rows = lax.all_to_all(out, ("x", "y"), 0, 0, tiled=True).reshape(SLOTS, -1)
        gram, score = products(rows, project, gram, score, start, length, prefix)
        arrived.append(rows)
        grams.append(gram)
    return finish(gram, score, arrived, place)


def shards(images, routes, orientations, groups, counts, defocus, projections):
    project = projections[0]
    where = jnp.stack([lax.axis_index("row"), lax.axis_index("z")]).astype(i32)
    zkey, place, code, select, most = make_plan(routes, orientations, groups, counts)
    plan = (zkey, code, select)
    operands = (images, project, plan, place, where, defocus)
    if len(SIZES) == 1:
        return exchange(SIZES[0], *operands)
    top = most_everywhere(most)[0, 0]
    index = sum((top > size).astype(i32) for size in SIZES[:-1])
    return lax.switch(index, [functools.partial(exchange, size) for size in SIZES], *operands)


def solution(mesh):
    split = Mesh(mesh.devices.reshape(4, 4, 8, 2), ("x", "y", "z", "row"))
    pose = ("x", "y", "z")
    in_specs = (P(pose, "row"), P(pose, None), P(pose), P(pose), P(pose), P(), P(pose, None, "row"))
    out_specs = (P(pose, None), P(pose, "row", None))
    return jax.shard_map(shards, mesh=split, in_specs=in_specs, out_specs=out_specs, check_vma=False)
```

```python
import functools

import jax
import jax.numpy as jnp
from jax import lax
from jax.experimental import pallas as pl
from jax.experimental.pallas import tpu as pltpu
from jax.sharding import Mesh, PartitionSpec as P

BOX = 256
K = 16
ORIENT = 4
GROUPS = 8
PANEL = 64
ROWS = 128
NZ = 8
NXY = 16
SLOTS = 256
HALF = 32768
TILE = 4096
SUB = 512
PREFIX = 128
CHUNKS = ((0, 4096), (4096, 4096), (8192, 8192), (16384, 8192), (24576, 4096), (28672, 4096))
SIZES = (20, 24, 32)

bf16, f32, i32 = jnp.bfloat16, jnp.float32, jnp.int32
HIGH = lax.Precision.HIGHEST
VMEM_LIMIT = 50 * 1024 * 1024


def iota(shape, axis):
    return lax.broadcasted_iota(i32, shape, axis)


def plan_kernel(count_ref, route_ref, orient_ref, group_ref, zkey_ref, place_ref, code_ref, select_ref, most_ref):
    count = count_ref[0]
    first = iota((ROWS, ROWS), 0)
    second = iota((ROWS, ROWS), 1)
    diagonal = first == second

    def column(row):
        return jnp.sum(jnp.where(diagonal, row, 0), axis=1, keepdims=True)

    route = route_ref[...]
    plane, block_xy = route & 7, route >> 3
    route_c = column(route)
    earlier = (first < second) & (first < count)
    rank = jnp.sum(jnp.where(earlier & (route_c == route), 1, 0), axis=0, keepdims=True)
    depth = jnp.sum(jnp.where(earlier & ((route_c & 7) == plane), 1, 0), axis=0, keepdims=True)
    live = iota((1, ROWS), 1) < count
    zkey_ref[...] = jnp.where(live, plane * 32 + depth, -1)
    place_ref[...] = jnp.where(live, route * 2 + rank, -1)
    code = (block_xy * 2 + rank) * ORIENT + orient_ref[...] + 1
    code_ref[...] = jnp.broadcast_to(column(code), (ROWS, ROWS)).astype(f32).astype(bf16)
    select_ref[...] = jnp.where(column(group_ref[...]) == second, 1.0, 0.0)
    most = jnp.max(jnp.where(live, depth + 1, 0), axis=1, keepdims=True)
    most_ref[...] = jnp.broadcast_to(most, (1, ROWS))


def make_plan(routes, orientations, groups, counts):
    vmem = pl.BlockSpec(memory_space=pltpu.VMEM)
    smem = pl.BlockSpec(memory_space=pltpu.SMEM)
    return pl.pallas_call(
        plan_kernel,
        out_shape=(
            jax.ShapeDtypeStruct((1, ROWS), i32),
            jax.ShapeDtypeStruct((1, ROWS), i32),
            jax.ShapeDtypeStruct((ROWS, ROWS), bf16),
            jax.ShapeDtypeStruct((ROWS, ROWS), f32),
            jax.ShapeDtypeStruct((1, ROWS), i32),
        ),
        in_specs=[smem, vmem, vmem, vmem],
        out_specs=(vmem,) * 5,
        cost_estimate=pl.CostEstimate(flops=2**21, bytes_accessed=2**18, transcendentals=0),
        name="plan",
    )(counts, routes.reshape(1, ROWS), orientations.reshape(1, ROWS), groups.reshape(1, ROWS))


def prep_kernel(start, prefix, extra, where_ref, defocus_ref, image_ref, zkey_ref, code_ref, select_ref, *refs):
    out_refs = refs[-NZ:]
    row_at, z_at = where_ref[0], where_ref[1]
    folds = 16 // extra if extra else 1
    span = TILE // folds
    tile_at = pl.program_id(0) * TILE
    line = iota((ROWS, ROWS), 0)
    target = ((z_at + (line >> 4)) & 7) * 32
    slot = line & 15
    zkey = zkey_ref[...]
    base = (zkey == target + slot)
    stack = [base]
    if extra:
        late = zkey == target + 16 + lax.rem(slot, extra)
        fold_of = lax.div(slot, extra)
    placers = []
    for fold in range(folds):
        parts = [base] + ([late & (fold_of == fold)] if extra else [])
        placers.append(jnp.where(jnp.concatenate(parts, 0), 1.0, 0.0).astype(bf16) if extra else jnp.where(base, 1.0, 0.0).astype(bf16))
    first_pixel = row_at * HALF + start + tile_at
    group = iota((GROUPS, SUB), 0)
    phase = jnp.zeros((GROUPS, SUB), f32)
    for g in range(GROUPS):
        phase = jnp.where(group == g, defocus_ref[g], phase)
    lane = iota((1, SUB), 1)

    def weighted(at):
        pixel = first_pixel + at + lane
        up = ((pixel >> 8) - BOX // 2).astype(f32)
        across = ((pixel & (BOX - 1)) - BOX // 2).astype(f32)
        radius = (up * up + across * across) / f32(BOX * BOX)
        table = jnp.sin(phase * radius)
        ctf = jnp.dot(select_ref[:, :GROUPS], table, precision=HIGH, preferred_element_type=f32)
        return (image_ref[:, at : at + SUB].astype(f32) * ctf).astype(bf16)

    head = PREFIX if prefix else 0
    if prefix:
        codes = code_ref[...]
        front = jnp.dot(placers[0], codes, preferred_element_type=f32).astype(bf16)
        for k in range(NZ):
            block = front[k * 16 : k * 16 + 16]
            if extra:
                block = jnp.where(iota((16, PREFIX), 1) < PREFIX // 2, block, front[ROWS + k * 16 : ROWS + k * 16 + 16])
            out_refs[k][:, 0:PREFIX] = block
    for offset in range(0, span, SUB):
        total = None
        for fold in range(folds):
            at = fold * span + offset
            placed = jnp.dot(placers[fold], weighted(at), preferred_element_type=f32)
            for k in range(NZ):
                out_refs[k][:, head + at : head + at + SUB] = placed[k * 16 : k * 16 + 16].astype(bf16)
            if extra:
                part = placed[ROWS:]
                total = part if total is None else total + part
        if extra:
            for k in range(NZ):
                at = head + TILE + offset
                out_refs[k][:, at : at + SUB] = total[k * 16 : k * 16 + 16].astype(bf16)


def width_of(extra):
    return TILE + TILE * extra // 16


def prep(images, plan, where, defocus, after, start, size, prefix, extra):
    zkey, code, select = plan
    tiles = size // TILE
    width = width_of(extra) + (PREFIX if prefix else 0)
    assert not prefix or tiles == 1
    smem = pl.BlockSpec(memory_space=pltpu.SMEM)
    whole = lambda shape: pl.BlockSpec(shape, lambda t: (0, 0))
    return pl.pallas_call(
        functools.partial(prep_kernel, start, prefix, extra),
        out_shape=(jax.ShapeDtypeStruct((16, tiles * width), bf16),) * NZ,
        grid=(tiles,),
        in_specs=[
            smem,
            smem,
            pl.BlockSpec((ROWS, TILE), lambda t: (0, start // TILE + t)),
            whole((1, ROWS)),
            whole((ROWS, ROWS)),
            whole((ROWS, ROWS)),
        ]
        + [pl.BlockSpec(memory_space=pl.ANY)] * len(after),
        out_specs=(pl.BlockSpec((16, width), lambda t: (0, t)),) * NZ,
        compiler_params=pltpu.CompilerParams(vmem_limit_bytes=VMEM_LIMIT),
        cost_estimate=pl.CostEstimate(flops=2**35, bytes_accessed=tiles * 2**21, transcendentals=0),
        name="prep",
    )(where, defocus, images, zkey, code, select, *after)


def spread_kernel(prefix, extra, *refs):
    folds = 16 // extra if extra else 1
    span = TILE // folds
    head = PREFIX if prefix else 0
    if prefix:
        where_ref, piece_refs, (out_ref, placer_ref) = refs[0], refs[1 : 1 + NZ], refs[-2:]
        z_at = where_ref[1]
        codes = jnp.concatenate([ref[:, 0:PREFIX] for ref in piece_refs], 0).astype(f32)
        line = iota((ROWS, SLOTS), 0)
        owner_slot = iota((ROWS, SLOTS), 1)
        source_z = (z_at - (line >> 4)) & 7
        halves = []
        for half in range(2 if extra else 1):
            code = codes[:, half * (PREFIX // 2) : half * (PREFIX // 2) + 1].astype(i32)
            if half:
                filled = (code > 0) & ((iota((ROWS, 1), 0) & 15) < extra)
            else:
                filled = code > 0
            ticket = code - 1
            slot = (ticket >> 3) * 16 + source_z * 2 + ((ticket >> 2) & 1)
            hit = filled & (slot == owner_slot)
            halves.append(jnp.where(hit, 1.0, 0.0).T)
        placer = jnp.concatenate(halves, 1) if extra else halves[0]
        placer_ref[...] = placer.astype(bf16)
    else:
        placer_in, piece_refs, out_ref = refs[0], refs[1 : 1 + NZ], refs[-1]
        placer = placer_in[...].astype(f32)
    base = placer[:, :ROWS].astype(bf16)
    if prefix:
        lanes = iota((ROWS, PREFIX), 1)
        early = jnp.concatenate([ref[:, 0:PREFIX] for ref in piece_refs], 0).astype(f32)
        front = jnp.dot(base, jnp.broadcast_to(early[:, 0:1], (ROWS, PREFIX)).astype(bf16), preferred_element_type=f32)
        if extra:
            late = placer[:, ROWS:].astype(bf16)
            later = jnp.broadcast_to(early[:, PREFIX // 2 : PREFIX // 2 + 1], (ROWS, PREFIX)).astype(bf16)
            front = front + jnp.dot(late, later, preferred_element_type=f32)
        out_ref[:, :, 0:PREFIX] = front.astype(bf16).reshape(NXY, 16, PREFIX)
    spread = []
    if extra:
        late = placer[:, ROWS:]
        column = iota((ROWS, ROWS), 1)
        row = iota((ROWS, ROWS), 0)
        for fold in range(folds):
            move = (column == (row & ~15) + fold * extra + (row & 15)) & ((row & 15) < extra)
            spread.append(jnp.dot(late.astype(bf16), jnp.where(move, 1.0, 0.0).astype(bf16), preferred_element_type=f32).astype(bf16))
    for fold in range(folds):
        for offset in range(0, span, SUB):
            at = fold * span + offset
            piece = jnp.concatenate([ref[:, head + at : head + at + SUB] for ref in piece_refs], 0)
            out = jnp.dot(base, piece, preferred_element_type=f32)
            if extra:
                lat = head + TILE + offset
                piece = jnp.concatenate([ref[:, lat : lat + SUB] for ref in piece_refs], 0)
                out = out + jnp.dot(spread[fold], piece, preferred_element_type=f32)
            out_ref[:, :, head + at : head + at + SUB] = out.astype(bf16).reshape(NXY, 16, SUB)


def spread(pieces, control, after, size, prefix, extra):
    tiles = size // TILE
    head = PREFIX if prefix else 0
    width = width_of(extra) + head
    columns = ROWS * 2 if extra else ROWS
    out_shape = jax.ShapeDtypeStruct((NXY, 16, size + head), bf16)
    out_spec = pl.BlockSpec((NXY, 16, TILE + head), lambda t: (0, 0, t))
    placer_spec = pl.BlockSpec((SLOTS, columns), lambda t: (0, 0))
    return pl.pallas_call(
        functools.partial(spread_kernel, prefix, extra),
        out_shape=(out_shape, jax.ShapeDtypeStruct((SLOTS, columns), bf16)) if prefix else out_shape,
        grid=(tiles,),
        in_specs=[pl.BlockSpec(memory_space=pltpu.SMEM) if prefix else placer_spec]
        + [pl.BlockSpec((16, width), lambda t: (0, t))] * NZ
        + [pl.BlockSpec(memory_space=pl.ANY)] * len(after),
        out_specs=(out_spec, placer_spec) if prefix else out_spec,
        compiler_params=pltpu.CompilerParams(vmem_limit_bytes=VMEM_LIMIT),
        cost_estimate=pl.CostEstimate(flops=2**36, bytes_accessed=tiles * 2**22, transcendentals=0),
        name="spread",
    )(control, *pieces, *after)


def products_kernel(head, rows_ref, project_ref, gram_in, score_in, gram_ref, score_ref):
    @pl.when(pl.program_id(0) == 0)
    def _():
        gram_ref[...] = gram_in[...]
        score_ref[...] = score_in[...]

    rows = rows_ref[:, head:]
    contract = (((1,), (1,)), ((), ()))
    gram_ref[...] += lax.dot_general(rows, rows, contract, preferred_element_type=f32)
    score_ref[...] += lax.dot_general(rows, project_ref[...], contract, preferred_element_type=f32)


def products(rows, project, gram, score, start, size, prefix):
    tiles = size // TILE
    head = PREFIX if prefix else 0
    whole = lambda shape: pl.BlockSpec(shape, lambda t: (0, 0))
    return pl.pallas_call(
        functools.partial(products_kernel, head),
        out_shape=(jax.ShapeDtypeStruct((SLOTS, SLOTS), f32), jax.ShapeDtypeStruct((SLOTS, K), f32)),
        grid=(tiles,),
        in_specs=[
            pl.BlockSpec((SLOTS, TILE + head), lambda t: (0, t)),
            pl.BlockSpec((K, TILE), lambda t: (0, start // TILE + t)),
            whole((SLOTS, SLOTS)),
            whole((SLOTS, K)),
        ],
        out_specs=(whole((SLOTS, SLOTS)), whole((SLOTS, K))),
        compiler_params=pltpu.CompilerParams(vmem_limit_bytes=VMEM_LIMIT),
        cost_estimate=pl.CostEstimate(flops=2**36, bytes_accessed=tiles * 2**21, transcendentals=0),
        name="products",
    )(rows, project, gram, score)


def weights_of(score, code):
    ticket = code - 1
    orient = ticket & 3
    tiled = jnp.concatenate([score] * ORIENT, axis=1)
    panel_o = iota((SLOTS, PANEL), 1) >> 4
    return jnp.where((ticket >= 0) & (panel_o == orient), tiled, 0.0).astype(bf16)


def local_gram_kernel(score_ref, other_ref, front_ref, gram_ref, total_ref, weight_ref, local_ref):
    score = score_ref[...] + other_ref[...]
    total_ref[...] = score
    code = front_ref[:, 0:1].astype(f32).astype(i32)
    weight = weights_of(score, code)
    weight_ref[...] = weight
    wide = weight.astype(f32)
    middle = jnp.dot(gram_ref[...], wide, precision=HIGH, preferred_element_type=f32)
    local_ref[...] = lax.dot_general(wide, middle, (((0,), (0,)), ((), ())), precision=HIGH, preferred_element_type=f32)


def local_gram(score, other, first_rows, gram):
    whole = lambda shape: pl.BlockSpec(shape, lambda: (0, 0))
    return pl.pallas_call(
        local_gram_kernel,
        out_shape=(
            jax.ShapeDtypeStruct((SLOTS, K), f32),
            jax.ShapeDtypeStruct((SLOTS, PANEL), bf16),
            jax.ShapeDtypeStruct((PANEL, PANEL), f32),
        ),
        in_specs=[whole((SLOTS, K)), whole((SLOTS, K)), whole((SLOTS, PREFIX)), whole((SLOTS, SLOTS))],
        out_specs=(whole((SLOTS, K)), whole((SLOTS, PANEL)), whole((PANEL, PANEL))),
        compiler_params=pltpu.CompilerParams(vmem_limit_bytes=VMEM_LIMIT),
        cost_estimate=pl.CostEstimate(flops=2**27, bytes_accessed=2**19, transcendentals=0),
        name="local_gram",
    )(score, other, first_rows, gram)


def factor_kernel(gram_ref, weight_ref, mix_ref):
    gram = gram_ref[...]
    first = iota((PANEL, PANEL), 0)
    second = iota((PANEL, PANEL), 1)
    same = jnp.where(first == second, 1.0, 0.0)
    shift = 0.001 * jnp.sum(gram * same) / PANEL
    wide = jnp.concatenate([gram + shift * same, same], axis=1)
    line = iota((PANEL, 2 * PANEL), 0)
    lane = iota((1, 2 * PANEL), 1)
    for j in range(PANEL):
        row = wide[j : j + 1, :]
        pivot = wide[j : j + 1, j : j + 1]
        scaled = row * lax.rsqrt(pivot)
        inverse = 1.0 / pivot
        column = wide[:, j : j + 1] * inverse
        below = line > j
        wide = jnp.where(below, wide - column * row, jnp.where(line == j, scaled, wide))
    inverse_lower = wide[:, PANEL:]
    mix = lax.dot_general(
        inverse_lower, weight_ref[...].astype(f32), (((1,), (1,)), ((), ())), precision=HIGH, preferred_element_type=f32
    ) * f32(float(128 * BOX * BOX) ** 0.5)
    high = mix.astype(bf16)
    low = (mix - high.astype(f32)).astype(bf16)
    mix_ref[...] = jnp.concatenate([high, low], axis=0)


def factor(gram, weight):
    whole = lambda shape: pl.BlockSpec(shape, lambda: (0, 0))
    return pl.pallas_call(
        factor_kernel,
        out_shape=jax.ShapeDtypeStruct((2 * PANEL, SLOTS), bf16),
        in_specs=[whole((PANEL, PANEL)), whole((SLOTS, PANEL))],
        out_specs=whole((2 * PANEL, SLOTS)),
        cost_estimate=pl.CostEstimate(flops=2**23, bytes_accessed=2**17, transcendentals=0),
        name="factor",
    )(gram, weight)


def basis_kernel(mix_ref, *refs):
    row_refs, out_ref = refs[:-1], refs[-1]
    step = pl.program_id(0)
    mix = mix_ref[...]
    for (start, size), ref in zip(CHUNKS, row_refs):
        head = PREFIX if start == 0 else 0

        @pl.when((step >= start // TILE) & (step < (start + size) // TILE))
        def _(ref=ref, head=head):
            both = jnp.dot(mix, ref[:, head:], preferred_element_type=f32)
            out_ref[...] = (both[:PANEL] + both[PANEL:]).astype(bf16)


def make_basis(mix, chunks):
    specs = []
    for start, size in CHUNKS:
        head = PREFIX if start == 0 else 0
        first, count = start // TILE, size // TILE
        specs.append(pl.BlockSpec((SLOTS, TILE + head), lambda t, first=first, count=count: (0, jnp.clip(t - first, 0, count - 1))))
    return pl.pallas_call(
        basis_kernel,
        out_shape=jax.ShapeDtypeStruct((PANEL, HALF), bf16),
        grid=(HALF // TILE,),
        in_specs=[pl.BlockSpec((2 * PANEL, SLOTS), lambda t: (0, 0))] + specs,
        out_specs=pl.BlockSpec((PANEL, TILE), lambda t: (0, t)),
        compiler_params=pltpu.CompilerParams(vmem_limit_bytes=VMEM_LIMIT),
        cost_estimate=pl.CostEstimate(flops=2**31, bytes_accessed=2**24, transcendentals=0),
        name="basis",
    )(mix, *chunks)


def shift_z(block, k):
    if k == 0:
        return block
    return lax.ppermute(block, "z", [(i, (i + k) % NZ) for i in range(NZ)])


def swap_row(value):
    return lax.ppermute(value, "row", [(0, 1), (1, 0)])


def sum_everywhere(value):
    value = value + swap_row(value)
    for axis, size in (("z", 8), ("x", 4), ("y", 4)):
        step = 1
        while step < size:
            value = value + lax.ppermute(value, axis, [(i, i ^ step) for i in range(size)])
            step *= 2
    return value


def most_everywhere(value):
    for axis, size in (("z", 8), ("x", 4), ("y", 4)):
        step = 1
        while step < size:
            value = jnp.maximum(value, lax.ppermute(value, axis, [(i, i ^ step) for i in range(size)]))
            step *= 2
    return value


def finish(gram, score, arrived, place):
    front = arrived[0][:, :PREFIX]
    score, weight, local = local_gram(score, swap_row(score), front, gram)
    returned = lax.all_to_all(score.reshape(128, 2, K), ("x", "y", "z"), 0, 0, tiled=True).reshape(SLOTS, K)
    placer = (place.reshape(ROWS, 1) == jnp.arange(SLOTS)[None, :]).astype(f32)
    coords = jnp.dot(placer, returned, precision=HIGH)
    total = sum_everywhere(local)
    basis = make_basis(factor(total, weight), arrived)
    return coords, basis.T.reshape(1, HALF, PANEL)


def exchange(size, images, project, plan, place, where, defocus):
    extra = size - 16
    gram = jnp.zeros((SLOTS, SLOTS), f32)
    score = jnp.zeros((SLOTS, K), f32)
    arrived, done = [], []
    control = where
    made = {}
    outs = {}

    def make(at):
        if at < len(CHUNKS):
            start, length = CHUNKS[at]
            after = [outs[at - 2]] if at >= 2 else []
            made[at] = prep(images, plan, where, defocus, after, start, length, start == 0, extra)

    make(0)
    make(1)
    for at, (start, length) in enumerate(CHUNKS):
        prefix = start == 0
        pieces = [shift_z(made[at][k], k) for k in range(NZ)]
        after = [made[at + 1][0]] if at + 1 < len(CHUNKS) else []
        after += arrived[-1:] + ([done[at - 2]] if at >= 2 else [])
        out = spread(pieces, control, after, length, prefix, extra)
        if prefix:
            out, control = out
        outs[at] = out
        make(at + 2)
        rows = lax.all_to_all(out, ("x", "y"), 0, 0, tiled=True).reshape(SLOTS, -1)
        gram, score = products(rows, project, gram, score, start, length, prefix)
        arrived.append(rows)
        done.append(gram)
    return finish(gram, score, arrived, place)


def shards(images, routes, orientations, groups, counts, defocus, projections):
    project = projections[0]
    where = jnp.stack([lax.axis_index("row"), lax.axis_index("z")]).astype(i32)
    zkey, place, code, select, most = make_plan(routes, orientations, groups, counts)
    plan = (zkey, code, select)
    operands = (images, project, plan, place, where, defocus)
    if len(SIZES) == 1:
        return exchange(SIZES[0], *operands)
    top = most_everywhere(most)[0, 0]
    index = sum((top > size).astype(i32) for size in SIZES[:-1])
    return lax.switch(index, [functools.partial(exchange, size) for size in SIZES], *operands)


def solution(mesh):
    split = Mesh(mesh.devices.reshape(4, 4, 8, 2), ("x", "y", "z", "row"))
    pose = ("x", "y", "z")
    in_specs = (P(pose, "row"), P(pose, None), P(pose), P(pose), P(pose), P(), P(pose, None, "row"))
    out_specs = (P(pose, None), P(pose, "row", None))
    return jax.shard_map(shards, mesh=split, in_specs=in_specs, out_specs=out_specs, check_vma=False)
```
